256 devices in a mesh: layer: 64 (over z, x_lo, y), shot: 4 (over x_hi, core).
Axes of the slice: x: 4 (x_hi: 2, x_lo: 2; x = x_hi * 2 + x_lo), y: 4, z: 8, core: 2. Of those that a mesh axis runs over, the one named last changes fastest.
Arguments:
- residual_src: bfloat16 [8, 192, 48, 1536], P('shot', 'layer'), may hold values from -6 to 6
- src_plane: int32 [8], P('shot'), may hold values from 0 to 191
- src_shift: int32 [8], P('shot'), may hold values from 0 to 767
- profile: bfloat16 [8, 48, 1536], P('shot'), may hold values from -6 to 6
- mass: bfloat16 [192, 48, 768], P('layer'), may hold values from 0.049804688 to 1
- damping: bfloat16 [192, 48, 768], P('layer'), may hold values from 0.049804688 to 0.5
- panel: bfloat16 [64, 1536, 1536], P('layer', None, 'shot'), may hold values from -0.15625 to 0.15625
- transmission: float32 [64, 48, 1536], P('layer'), may hold values from -1 to 1, as said below
Outputs:
- solution: bfloat16 [8, 192, 48, 1536], P('shot', 'layer')
The draws below stay inside these ranges and needn't reach their ends.
Inputs may be any that keep to these rules, and one draw needn't show every extreme that they name: `transmission`: each cell's complex factor, real part in the first 768 columns and imaginary part in the last 768, has magnitude below one.
All inputs are finite; a program needn't handle non-finite values.
Results may differ from the reference program's by a relative error of at most 0.0045.
Values may be sent and summed in bfloat16 or wider, within the bound.
A program may use at most 192 MiB of HBM per device.

```python
import math
import jax
import jax.numpy as jnp
from jax import lax

NX = 768
NY = 48
LZ = 3
SWEEPS = 2
LAYER_GROUPS = 64
NZ = 192
SHOTS = 8


def draw_transmission(key, part):
    random_subkeys = jax.random.split(key, 5)
    rate_low = math.log(0.2 / LAYER_GROUPS)
    rate_high = math.log(1.5)
    baseline_rate = jnp.exp(jax.random.uniform(random_subkeys[0], (1, NY, NX), jnp.float32, rate_low, rate_high))
    spread_width = jnp.exp(jax.random.uniform(random_subkeys[1], (LAYER_GROUPS, NY, NX), jnp.float32, math.log(0.5), math.log(2.0)))
    spike_selection = jax.random.randint(random_subkeys[2], (LAYER_GROUPS, 1, 1), 0, 16) == 0
    spike_level = jax.random.uniform(random_subkeys[3], (LAYER_GROUPS, 1, 1), jnp.float32, 0.5, 0.8)
    spike_scale = jnp.where(spike_selection, spike_level, 1.0)
    smoothing_radius = jnp.exp(-baseline_rate * spread_width) * spike_scale
    angle_val = jax.random.uniform(random_subkeys[4], (LAYER_GROUPS, NY, NX), jnp.float32, -math.pi, math.pi)
    return jnp.concatenate([smoothing_radius * jnp.cos(angle_val), smoothing_radius * jnp.sin(angle_val)], axis=-1).astype(jnp.float32)


def set_ends(result, key, least, top_value):
    index_at = [jax.random.randint(jax.random.fold_in(key, axis), (), 0, length) for axis, length in enumerate(result.shape)]
    longest = result.shape.index(max(result.shape))
    neighbour = index_at[:longest] + [(index_at[longest] + 1) % result.shape[longest]] + index_at[longest + 1:]
    return result.at[tuple(index_at)].set(least).at[tuple(neighbour)].set(top_value)


def block_levels(own_key, shape, shards, smallest, high):
    level = 1.0
    for position, blocks in shards:
        steps = jax.random.uniform(jax.random.fold_in(jax.random.fold_in(own_key, 6), position), (blocks,), jnp.float32, smallest / len(shards), high / len(shards))
        level = level * jnp.repeat(jnp.exp(steps), shape[position] // blocks).reshape((-1,) + (1,) * (len(shape) - 1 - position))
    return level


def noise(key, dims, spread, most, shards=(), kind=jnp.bfloat16):
    entries = jax.random.normal(key, dims, jnp.float32) * spread
    if len(shards) > 0:
        entries = block_levels(key, dims, shards, -0.22, 0.18) * entries
    return jnp.clip(entries, min=-most, max=most).astype(kind)


def setup_inputs(seed: int = 0) -> dict:
    keys = jax.random.split(jax.random.key(seed), 9)
    return {
        "residual_src": noise(keys[0], (SHOTS, NZ, NY, 2 * NX), 1.0, 6.0, ((0, 4), (1, 64))),
        "src_plane": set_ends(jax.random.randint(keys[1], (SHOTS,), 0, NZ), jax.random.fold_in(keys[1], 1), 0, NZ - 1).astype(jnp.int32),
        "src_shift": set_ends(jax.random.randint(keys[2], (SHOTS,), 0, NX), jax.random.fold_in(keys[2], 1), 0, NX - 1).astype(jnp.int32),
        "profile": noise(keys[3], (SHOTS, NY, 2 * NX), 1.0, 6.0, ((0, 4),)),
        "mass": jnp.clip(jnp.exp(math.log(1.0) - 2.9996462 * jax.random.uniform(keys[4], (NZ, NY, NX), jnp.float32) ** block_levels(keys[4], (NZ, NY, NX), ((0, 64),), -0.2, 0.2)), 0.049804688, 1.0).astype(jnp.bfloat16),
        "damping": jnp.clip(jnp.exp(math.log(0.5) - 2.306499 * jax.random.uniform(keys[5], (NZ, NY, NX), jnp.float32) ** block_levels(keys[5], (NZ, NY, NX), ((0, 64),), -0.2, 0.2)), 0.049804688, 0.5).astype(jnp.bfloat16),
        "panel": noise(keys[6], (LAYER_GROUPS, 2 * NX, 2 * NX), (2 * NX) ** -0.5, 0.15625, ((0, 64), (2, 4))),
        "transmission": draw_transmission(jax.random.fold_in(keys[8], 71), 0),
    }


relaxation = 0.8


def complex_mul(first_op, second_op):
    half_width = first_op.shape[-1] // 2
    real_one = first_op[..., :half_width]
    imag_one = first_op[..., half_width:]
    real_two = second_op[..., :half_width]
    imag_two = second_op[..., half_width:]
    return jnp.concatenate([real_one * real_two - imag_one * imag_two, real_one * imag_two + imag_one * real_two], axis=-1)


def lateral_smooth(values):
    half_width = values.shape[-1] // 2
    split_view = values.reshape(values.shape[:-1] + (2, half_width))
    padded = jnp.pad(split_view, [(0, 0)] * (split_view.ndim - 1) + [(1, 1)])
    along_x = 0.5 * padded[..., :-2] + padded[..., 1:-1] + 0.5 * padded[..., 2:]
    along_x = along_x.reshape(values.shape)
    padded_y = jnp.pad(along_x, [(0, 0)] * (values.ndim - 2) + [(1, 1), (0, 0)])
    return 0.5 * padded_y[..., :-2, :] + padded_y[..., 1:-1, :] + 0.5 * padded_y[..., 2:, :]


def depth_smooth(padded, axis_pos):
    inner_count = padded.shape[axis_pos] - 2
    above_part = lax.slice_in_dim(padded, 0, inner_count, axis=axis_pos)
    middle = lax.slice_in_dim(padded, 1, inner_count + 1, axis=axis_pos)
    below_part = lax.slice_in_dim(padded, 2, inner_count + 2, axis=axis_pos)
    return 0.5 * above_part + middle + 0.5 * below_part


def coefficients(mass_val, damp_val):
    shifted = 1.0 + mass_val
    modulus = shifted * shifted + damp_val * damp_val
    diag_coef = jnp.concatenate([shifted, damp_val], axis=-1)
    inverse = jnp.concatenate([shifted / modulus, -damp_val / modulus], axis=-1)
    return diag_coef, inverse


def jacobi_update(iterate, smoothed, source_field, diag_coef, inverse):
    residual_now = source_field - complex_mul(diag_coef, iterate) + (smoothed - iterate) / 7.0
    return iterate + relaxation * complex_mul(inverse, residual_now)


def reference(residual_src, src_plane, src_shift, profile, mass, damping, panel, transmission):
    panel_wide = panel.astype(jnp.float32)
    diag_coef, inverse = coefficients(mass.astype(jnp.float32), damping.astype(jnp.float32))
    depth_ids = jnp.arange(NZ, dtype=jnp.int32)

    def one_shot(shot_data):
        shot_src, plane_id, shift_id, shot_profile = shot_data
        shifted_profile = jnp.roll(shot_profile.astype(jnp.float32).reshape(NY, 2, NX), shift_id, axis=2).reshape(NY, 2 * NX)
        on_plane = (depth_ids == plane_id).astype(jnp.float32)
        forcing = (shot_src.astype(jnp.float32) + on_plane[:, None, None] * shifted_profile[None]).astype(jnp.bfloat16)
        grouped = forcing.reshape(LAYER_GROUPS, LZ * NY, 2 * NX).astype(jnp.float32)
        panel_field = grouped + jnp.einsum("gra,gab->grb", grouped, panel_wide, precision=lax.Precision.HIGHEST)
        panel_field = panel_field.reshape(LAYER_GROUPS, LZ, NY, 2 * NX)
        bottoms = panel_field[:, LZ - 1]

        def advance(carried, pair_in):
            factor, bottom_trace = pair_in
            return complex_mul(factor, carried) + bottom_trace, carried

        _, incoming = lax.scan(advance, jnp.zeros((NY, 2 * NX), jnp.float32), (transmission, bottoms))
        source_field = jnp.concatenate([panel_field[:, :1] + incoming[:, None], panel_field[:, 1:]], axis=1)
        source_field = source_field.reshape(NZ, NY, 2 * NX)
        iterate = relaxation * complex_mul(inverse, source_field)
        for sweep_no in range(SWEEPS - 1):
            padded = jnp.pad(iterate, ((1, 1), (0, 0), (0, 0)))
            smoothed = depth_smooth(lateral_smooth(padded), 0)
            iterate = jacobi_update(iterate, smoothed, source_field, diag_coef, inverse)
        return iterate.astype(jnp.bfloat16)

    return lax.map(one_shot, (residual_src, src_plane, src_shift, profile))
```

```python
import jax
import jax.numpy as jnp
from jax import lax
from jax.experimental import pallas as pl
from jax.experimental.pallas import tpu as pltpu
from jax.sharding import PartitionSpec as P

MESH = pl.DeviceIdType.MESH
F32, BF16 = jnp.float32, jnp.bfloat16
RELAX = 0.8
NY, NX, W, LZ = 48, 768, 1536, 3
ROWS = 2 * NY
COLS = 384
HALF = 384
NT = 9
NPOS = 16


def forcing_kernel(plane_ref, shift_ref, res_ref, prof_ref, out_ref):
    first = lax.axis_index("layer") * LZ
    for shot in range(2):
        rows = pl.ds(shot * NY, NY)
        for p in range(LZ):
            out_ref[p, rows] = res_ref[shot, p]
        at = plane_ref[shot] - first

        @pl.when((at >= 0) & (at < LZ))
        def _():
            for half in range(2):
                cols = pl.ds(half * NX, NX)
                rolled = pltpu.roll(prof_ref[shot, :, cols].astype(F32), shift_ref[shot], axis=1)
                out_ref[at, rows, cols] = (res_ref[shot, at, :, cols].astype(F32) + rolled).astype(BF16)


def cmul(ar, ai, br, bi):
    return ar * br - ai * bi, ar * bi + ai * br


def lateral(w):
    col = lax.broadcasted_iota(jnp.int32, w.shape, 1)
    row = lax.broadcasted_iota(jnp.int32, w.shape, 0)
    left = jnp.where(col == 0, 0.0, pltpu.roll(w, 1, axis=1))
    right = jnp.where(col == w.shape[1] - 1, 0.0, pltpu.roll(w, w.shape[1] - 1, axis=1))
    w = w + 0.5 * (left + right)
    up = jnp.where(row == 0, 0.0, pltpu.roll(w, 1, axis=0))
    down = jnp.where(row == w.shape[0] - 1, 0.0, pltpu.roll(w, w.shape[0] - 1, axis=0))
    return w + 0.5 * (up + down)


def sweep_kernel(
    f_hbm, mass_hbm, damp_hbm, panel_hbm, trans_hbm, out_hbm,
    pan, fa, rs, rr, md, coef, tv, ty, tblk, ttile, ot,
    pf2, bq, by, tot, ob, ibs, inb, ins, inc, va, hs, hr, outv,
    loc, f_s, f_r, r_s, r_r, md_s, md_r, ty_s, ty_r, tt_s, tt_r,
    by_s, by_r, tot_s, tot_r, ib_s, ib_r, in_s, in_r, h_s, h_r, out_s,
):
    layer, s = lax.axis_index("layer"), lax.axis_index("shot")
    nl = 64
    z, xl, y = layer // 8, (layer // 4) % 2, layer % 4
    xh, core = s // 2, s % 2
    pos = layer // 4

    def rel(k):
        c = (core + k % 2) % 2
        x = (xh + k // 2) % 2
        return x * 2 + c

    def shot_dev(k):
        return (layer, rel(k))

    def y_at(d):
        return (y + d) % 4

    def y_dev(d):
        return ((layer // 4) * 4 + y_at(d), s)

    def pos_dev(p):
        return (p * 4 + y, s)

    def owner(t):
        zt = t % 8
        return zt * 2 + (t + t // 8 + core) % 2

    has_low = (z + core) % 2 == xl
    own_tile = jnp.where(has_low, z, 8)
    owns = has_low | (z == 0)

    up_dev = ((layer + 1) % nl, s)
    dn_dev = ((layer + nl - 1) % nl, s)

    def remote(src, dst, ss, rsem, dev):
        return pltpu.make_async_remote_copy(
            src_ref=src, dst_ref=dst, send_sem=ss, recv_sem=rsem, device_id=dev, device_id_type=MESH
        )

    my_half = pl.multiple_of((y % 2) * HALF, 128)
    loads = [
        pltpu.make_async_copy(panel_hbm.at[0], pan, loc.at[0]),
        pltpu.make_async_copy(f_hbm, fa.at[0], loc.at[1]),
        pltpu.make_async_copy(trans_hbm.at[0], tv, loc.at[2]),
        pltpu.make_async_copy(mass_hbm, md.at[0, pl.ds(0, LZ)], loc.at[3]),
        pltpu.make_async_copy(damp_hbm, md.at[1, pl.ds(0, LZ)], loc.at[4]),
        pltpu.make_async_copy(trans_hbm.at[0, :, pl.ds(my_half, HALF)], ty.at[y, 0], loc.at[5]),
        pltpu.make_async_copy(trans_hbm.at[0, :, pl.ds(NX + my_half, HALF)], ty.at[y, 1], loc.at[6]),
    ]
    for c in loads:
        c.start()

    barrier = pltpu.get_barrier_semaphore()
    greet = [shot_dev(k) for k in (1, 2, 3)] + [y_dev(d) for d in (1, 2, 3)]
    greet += [up_dev, dn_dev]
    greet += [pos_dev((pos + d) % NPOS) for d in range(1, NPOS)]
    for dev in greet:
        pl.semaphore_signal(barrier, inc=1, device_id=dev, device_id_type=MESH)
    pl.semaphore_wait(barrier, len(greet))

    def f_partner(p):
        return remote(f_hbm.at[p], fa.at[2, p], f_s.at[p, 1], f_r.at[p, 1], shot_dev(2))

    def f_sibling(p):
        return remote(f_hbm.at[p], fa.at[1, p], f_s.at[p, 0], f_r.at[p, 0], shot_dev(1))

    def f_forward(p):
        return remote(fa.at[2, p], fa.at[3, p], f_s.at[p, 2], f_r.at[p, 2], shot_dev(1))

    def r_back(p, k):
        return remote(rs.at[k, p], rr.at[p, s], r_s.at[p, k - 1], r_r.at[p, k - 1], shot_dev(k))

    order = (2, 0, 1)
    f_partner(2).start()
    for p in order:
        f_sibling(p).start()

    def t_send(d):
        off = pl.multiple_of((y_at(d) % 2) * HALF, 128)
        return [
            remote(trans_hbm.at[0, :, pl.ds(off + part * NX, HALF)], ty.at[y, part],
                   ty_s.at[d - 1, part], ty_r.at[d - 1, part], y_dev(d))
            for part in range(2)
        ]

    t_sends = [c for d in (1, 2, 3) for c in t_send(d)]
    for c in t_sends:
        c.start()
    md_sends = [
        remote(mass_hbm.at[0], md.at[0, LZ], md_s.at[0], md_r.at[0], dn_dev),
        remote(damp_hbm.at[0], md.at[1, LZ], md_s.at[1], md_r.at[1], dn_dev),
    ]
    for c in md_sends:
        c.start()

    loads[0].wait()
    loads[1].wait()

    def product(slot, planes):
        lhs = fa[slot, planes]
        m = lhs.shape[0] * ROWS if lhs.ndim == 3 else ROWS
        return jnp.dot(lhs.reshape(m, W), pan[...], preferred_element_type=F32).astype(BF16)

    own = product(0, slice(0, LZ))
    for p in range(LZ):
        rr[p, s] = own[p * ROWS:(p + 1) * ROWS]
    for p in order:
        f_sibling(p).wait_recv()
    sib = product(1, slice(0, LZ))
    for p in order:
        rs[1, p] = sib[p * ROWS:(p + 1) * ROWS]
        r_back(p, 1).start()

    loads[3].wait()
    loads[4].wait()

    def coefficients(p):
        sh = 1.0 + md[0, p].astype(F32)
        dm = md[1, p].astype(F32)
        w = RELAX / (sh * sh + dm * dm)
        coef[p, 0] = w * sh
        coef[p, 1] = -(w * dm)

    for p in range(LZ):
        coefficients(p)

    def exchange(p, following):
        f_partner(p).wait_recv()
        if following is not None:
            f_partner(p).wait_send()
            f_partner(following).start()
        f_forward(p).start()
        rs[2, p] = product(2, p)
        r_back(p, 2).start()
        f_forward(p).wait_recv()
        rs[3, p] = product(3, p)
        r_back(p, 3).start()

    exchange(2, 0)

    loads[2].wait()
    loads[5].wait()
    loads[6].wait()
    for c in t_sends:
        c.wait_recv()
    tr, ti = ty[0, 0], ty[0, 1]
    for j in range(1, 4):
        tr, ti = cmul(ty[j, 0], ty[j, 1], tr, ti)
    tblk[0] = tr
    tblk[1] = ti
    for t in range(NT):
        rt, ct = pl.ds((t // 3) * 16, 16), pl.ds((t % 3) * 128, 128)
        for part in range(2):
            ttile[t, part] = tblk[part, rt, ct]

    def tile_send(t, src, dst, ss, rsem):
        @pl.when(owner(t) != pos)
        def _():
            remote(src.at[t], dst.at[pos], ss.at[t], rsem.at[pos], pos_dev(owner(t))).start()

        @pl.when(owner(t) == pos)
        def _():
            dst[pos] = src[t]

    def tile_sent(t, src, dst, ss, rsem):
        @pl.when(owner(t) != pos)
        def _():
            remote(src.at[t], dst.at[pos], ss.at[t], rsem.at[pos], pos_dev(owner(t))).wait_send()

    def tile_recv(src, dst, ss, rsem):
        for q in range(NPOS):
            @pl.when(pos != q)
            def _():
                remote(src.at[0], dst.at[q], ss.at[0], rsem.at[q], pos_dev(q)).wait_recv()

    for t in range(NT):
        tile_send(t, ttile, ot, tt_s, tt_r)

    def field(p, shot, part):
        rows = pl.ds(shot * NY, NY)
        f = fa[0, p, rows, pl.ds(part * NX, NX)].astype(F32)
        prod = jnp.concatenate([rr[p, part * 2, rows], rr[p, part * 2 + 1, rows]], axis=-1)
        return f + prod.astype(F32)

    for k in (1, 2, 3):
        r_back(2, k).wait_recv()
    for shot in range(2):
        rows = pl.ds(shot * NY, NY)
        re, im = field(2, shot, 0), field(2, shot, 1)
        pf2[rows, pl.ds(0, NX)] = re
        pf2[rows, pl.ds(NX, NX)] = im
        for c in range(2):
            cut = slice(c * HALF, (c + 1) * HALF)
            bq[shot * 2 + c, :, pl.ds(0, HALF)] = re[:, cut].astype(BF16)
            bq[shot * 2 + c, :, pl.ds(HALF, HALF)] = im[:, cut].astype(BF16)

    def b_send(d):
        return remote(bq.at[y_at(d)], by.at[y], by_s.at[d - 1], by_r.at[d - 1], y_dev(d))

    for d in (1, 2, 3):
        b_send(d).start()
    by[y] = bq[y]

    def local_iterate(p, slot):
        for shot in range(2):
            rows = pl.ds(shot * NY, NY)
            if p == 2:
                re, im = pf2[rows, pl.ds(0, NX)], pf2[rows, pl.ds(NX, NX)]
            else:
                re, im = field(p, shot, 0), field(p, shot, 1)
            vr, vi = cmul(coef[p, 0], coef[p, 1], re, im)
            va[p + 1, rows, pl.ds(0, NX)] = vr
            va[p + 1, rows, pl.ds(NX, NX)] = vi
            if slot is not None:
                hs[slot, rows, pl.ds(0, NX)] = vr.astype(BF16)
                hs[slot, rows, pl.ds(NX, NX)] = vi.astype(BF16)

    local_iterate(2, 0)
    halo_down = remote(hs.at[0], hr.at[0], h_s.at[0], h_r.at[0], up_dev)
    halo_up = remote(hs.at[1], hr.at[1], h_s.at[1], h_r.at[1], dn_dev)
    halo_down.start()

    exchange(0, 1)

    for d in (1, 2, 3):
        b_send(d).wait_recv()
    re, im = by[0, :, pl.ds(0, HALF)].astype(F32), by[0, :, pl.ds(HALF, HALF)].astype(F32)
    for j in range(1, 4):
        re, im = cmul(ty[j, 0], ty[j, 1], re, im)
        re = re + by[j, :, pl.ds(0, HALF)].astype(F32)
        im = im + by[j, :, pl.ds(HALF, HALF)].astype(F32)
    for t in range(NT):
        rt, ct = slice((t // 3) * 16, (t // 3) * 16 + 16), slice((t % 3) * 128, (t % 3) * 128 + 128)
        tot[t, 0] = re[rt, ct].astype(BF16)
        tot[t, 1] = im[rt, ct].astype(BF16)
    for t in range(NT):
        tile_send(t, tot, ob, tot_s, tot_r)

    for k in (1, 2, 3):
        r_back(0, k).wait_recv()
    local_iterate(0, 1)
    halo_up.start()

    exchange(1, None)

    def back(q):
        return remote(ibs.at[q], inb.at[own_tile], ib_s.at[q], ib_r.at[own_tile], pos_dev(q))

    @pl.when(owns)
    def _():
        tile_recv(ttile, ot, tt_s, tt_r)
        tile_recv(tot, ob, tot_s, tot_r)
        cr = jnp.zeros((16, 128), F32)
        ci = jnp.zeros((16, 128), F32)
        for q in range(NPOS):
            ibs[q, 0] = cr.astype(BF16)
            ibs[q, 1] = ci.astype(BF16)

            @pl.when(pos != q)
            def _():
                back(q).start()

            if q < NPOS - 1:
                cr, ci = cmul(ot[q, 0], ot[q, 1], cr, ci)
                cr = cr + ob[q, 0].astype(F32)
                ci = ci + ob[q, 1].astype(F32)
        inb[own_tile] = ibs[pos]

    for k in (1, 2, 3):
        r_back(1, k).wait_recv()
    local_iterate(1, None)

    for c in md_sends:
        c.wait_recv()
    coefficients(LZ)

    for t in range(NT):
        @pl.when(owner(t) != pos)
        def _():
            remote(ibs.at[0], inb.at[t], ib_s.at[0], ib_r.at[t], pos_dev(owner(t))).wait_recv()
    parts = [
        jnp.concatenate(
            [jnp.concatenate([inb[rt * 3 + ct, part] for ct in range(3)], axis=-1) for rt in range(3)], axis=0
        ).astype(F32)
        for part in range(2)
    ]
    re, im = parts
    for j in range(4):
        ins[j, :, pl.ds(0, HALF)] = re.astype(BF16)
        ins[j, :, pl.ds(HALF, HALF)] = im.astype(BF16)
        if j < 3:
            re, im = cmul(ty[j, 0], ty[j, 1], re, im)
            re = re + by[j, :, pl.ds(0, HALF)].astype(F32)
            im = im + by[j, :, pl.ds(HALF, HALF)].astype(F32)

    def in_send(d):
        return remote(ins.at[y_at(d)], inc.at[y], in_s.at[d - 1], in_r.at[d - 1], y_dev(d))

    for d in (1, 2, 3):
        in_send(d).start()
    inc[y] = ins[y]

    halo_down.wait_recv()
    halo_up.wait_recv()
    not_first = jnp.where(layer == 0, 0.0, 1.0).astype(F32)
    not_last = jnp.where(layer == nl - 1, 0.0, 1.0).astype(F32)
    va[0] = hr[0].astype(F32) * not_first

    for d in (1, 2, 3):
        in_send(d).wait_recv()
    for shot in range(2):
        rows = pl.ds(shot * NY, NY)
        re = jnp.concatenate([inc[shot * 2 + c, :, pl.ds(0, HALF)] for c in range(2)], axis=-1).astype(F32)
        im = jnp.concatenate([inc[shot * 2 + c, :, pl.ds(HALF, HALF)] for c in range(2)], axis=-1).astype(F32)
        vr, vi = cmul(coef[0, 0], coef[0, 1], re, im)
        rcols, icols = pl.ds(0, NX), pl.ds(NX, NX)
        va[1, rows, rcols] += vr
        va[1, rows, icols] += vi
        nr, ni = cmul(tv[:, rcols], tv[:, icols], re, im)
        nr = nr + pf2[rows, rcols]
        ni = ni + pf2[rows, icols]
        vr, vi = cmul(coef[LZ, 0], coef[LZ, 1], nr, ni)
        va[4, rows, rcols] = (vr + hr[1, rows, rcols].astype(F32)) * not_last
        va[4, rows, icols] = (vi + hr[1, rows, icols].astype(F32)) * not_last

    outs = []
    for p in range(LZ):
        for shot in range(2):
            rows = pl.ds(shot * NY, NY)
            diff = []
            for part in range(2):
                cols = pl.ds(part * NX, NX)
                mid = va[p + 1, rows, cols]
                w = mid + 0.5 * (va[p, rows, cols] + va[p + 2, rows, cols])
                diff.append(lateral(w) - mid)
            dr, di = cmul(coef[p, 0], coef[p, 1], diff[0], diff[1])
            outv[shot, p, :, pl.ds(0, NX)] = (1.2 * va[p + 1, rows, pl.ds(0, NX)] + dr * (1.0 / 7.0)).astype(BF16)
            outv[shot, p, :, pl.ds(NX, NX)] = (1.2 * va[p + 1, rows, pl.ds(NX, NX)] + di * (1.0 / 7.0)).astype(BF16)
            c = pltpu.make_async_copy(outv.at[shot, p], out_hbm.at[shot, p], out_s.at[shot, p])
            c.start()
            outs.append(c)

    for p in order:
        if p == 1:
            f_partner(p).wait_send()
        f_sibling(p).wait_send()
        f_forward(p).wait_send()
        for k in (1, 2, 3):
            r_back(p, k).wait_send()
    for c in t_sends + md_sends + [halo_down, halo_up]:
        c.wait_send()
    for d in (1, 2, 3):
        b_send(d).wait_send()
        in_send(d).wait_send()
    for t in range(NT):
        tile_sent(t, ttile, ot, tt_s, tt_r)
        tile_sent(t, tot, ob, tot_s, tot_r)

    @pl.when(owns)
    def _():
        for q in range(NPOS):
            @pl.when(pos != q)
            def _():
                back(q).wait_send()

    for c in outs:
        c.wait()


def on_device(residual_src, src_plane, src_shift, profile, mass, damping, panel, transmission):
    vmem = pl.BlockSpec(memory_space=pltpu.VMEM)
    smem = pl.BlockSpec(memory_space=pltpu.SMEM)
    hbm = pl.BlockSpec(memory_space=pl.ANY)
    forcing = pl.pallas_call(
        forcing_kernel,
        out_shape=jax.ShapeDtypeStruct((LZ, ROWS, W), BF16),
        in_specs=[smem, smem, vmem, vmem],
        out_specs=vmem,
        name="forcing",
        compiler_params=pltpu.CompilerParams(vmem_limit_bytes=16 * 2**20),
    )(src_plane, src_shift, residual_src, profile)
    dma = pltpu.SemaphoreType.DMA
    scratch = [
        pltpu.VMEM((W, COLS), BF16),
        pltpu.VMEM((4, LZ, ROWS, W), BF16),
        pltpu.VMEM((4, LZ, ROWS, COLS), BF16),
        pltpu.VMEM((LZ, 4, ROWS, COLS), BF16),
        pltpu.VMEM((2, LZ + 1, NY, NX), BF16),
        pltpu.VMEM((LZ + 1, 2, NY, NX), F32),
        pltpu.VMEM((NY, W), F32),
        pltpu.VMEM((4, 2, NY, HALF), F32),
        pltpu.VMEM((2, NY, HALF), F32),
        pltpu.VMEM((NT, 2, 16, 128), F32),
        pltpu.VMEM((NPOS, 2, 16, 128), F32),
        pltpu.VMEM((ROWS, W), F32),
        pltpu.VMEM((4, NY, NX), BF16),
        pltpu.VMEM((4, NY, NX), BF16),
        pltpu.VMEM((NT, 2, 16, 128), BF16),
        pltpu.VMEM((NPOS, 2, 16, 128), BF16),
        pltpu.VMEM((NPOS, 2, 16, 128), BF16),
        pltpu.VMEM((NT, 2, 16, 128), BF16),
        pltpu.VMEM((4, NY, NX), BF16),
        pltpu.VMEM((4, NY, NX), BF16),
        pltpu.VMEM((5, ROWS, W), F32),
        pltpu.VMEM((2, ROWS, W), BF16),
        pltpu.VMEM((2, ROWS, W), BF16),
        pltpu.VMEM((2, LZ, NY, W), BF16),
        dma((7,)), dma((LZ, 3)), dma((LZ, 3)), dma((LZ, 3)), dma((LZ, 3)), dma((2,)), dma((2,)),
        dma((3, 2)), dma((3, 2)), dma((NT,)), dma((NPOS,)),
        dma((3,)), dma((3,)), dma((NT,)), dma((NPOS,)), dma((NPOS,)), dma((NT,)),
        dma((3,)), dma((3,)), dma((2,)), dma((2,)), dma((2, LZ)),
    ]
    return pl.pallas_call(
        sweep_kernel,
        out_shape=jax.ShapeDtypeStruct((2, LZ, NY, W), BF16),
        in_specs=[hbm] * 5,
        out_specs=hbm,
        scratch_shapes=scratch,
        name="sweep",
        compiler_params=pltpu.CompilerParams(
            collective_id=0, has_side_effects=True, vmem_limit_bytes=40 * 2**20
        ),
    )(forcing, mass, damping, panel, transmission)


def solution(mesh):
    placed = (
        P("shot", "layer", None, None),
        P("shot"),
        P("shot"),
        P("shot", None, None),
        P("layer", None, None),
        P("layer", None, None),
        P("layer", None, "shot"),
        P("layer", None, None),
    )
    return jax.shard_map(
        on_device,
        mesh=mesh,
        in_specs=placed,
        out_specs=P("shot", "layer", None, None),
        check_vma=False,
    )
```

```python
import jax
import jax.numpy as jnp
from jax import lax
from jax.experimental import pallas as pl
from jax.experimental.pallas import tpu as pltpu
from jax.sharding import PartitionSpec as P

MESH = pl.DeviceIdType.MESH
F32, BF16 = jnp.float32, jnp.bfloat16
RELAX = 0.8
TT = BF16
NY, NX, W, LZ = 48, 768, 1536, 3
ROWS = 2 * NY
COLS = 384
HALF = 384
NT = 9
NPOS = 16


def rolled(x, shift):
    for k in range(10):
        x = jnp.where((shift >> k) & 1 == 1, pltpu.roll(x, 1 << k, axis=1), x)
    return x


def cmul(ar, ai, br, bi):
    return ar * br - ai * bi, ar * bi + ai * br


def lateral(w):
    col = lax.broadcasted_iota(jnp.int32, w.shape, 1)
    row = lax.broadcasted_iota(jnp.int32, w.shape, 0)
    left = jnp.where(col == 0, 0.0, pltpu.roll(w, 1, axis=1))
    right = jnp.where(col == w.shape[1] - 1, 0.0, pltpu.roll(w, w.shape[1] - 1, axis=1))
    w = w + 0.5 * (left + right)
    up = jnp.where(row == 0, 0.0, pltpu.roll(w, 1, axis=0))
    down = jnp.where(row == w.shape[0] - 1, 0.0, pltpu.roll(w, w.shape[0] - 1, axis=0))
    return w + 0.5 * (up + down)


def sweep_kernel(
    plane_ref, shift_ref, res_hbm, prof_hbm, mass_hbm, damp_hbm, panel_hbm, trans_hbm, out_hbm,
    resv, profv, pan, fa, rs, rr, md, coef, tv, ty, tblk, ttile, ot,
    pf2, bq, by, tot, ob, ibs, inb, ins, inc, va, hs, hr, outv,
    loc, f_s, f_r, r_s, r_r, md_s, md_r, ty_s, ty_r, tt_s, tt_r,
    by_s, by_r, tot_s, tot_r, ib_s, ib_r, in_s, in_r, h_s, h_r, out_s,
):
    layer, s = lax.axis_index("layer"), lax.axis_index("shot")
    nl = 64
    z, xl, y = layer // 8, (layer // 4) % 2, layer % 4
    xh, core = s // 2, s % 2
    pos = layer // 4

    def rel(k):
        c = (core + k % 2) % 2
        x = (xh + k // 2) % 2
        return x * 2 + c

    def shot_dev(k):
        return (layer, rel(k))

    def y_at(d):
        return (y + d) % 4

    def y_dev(d):
        return ((layer // 4) * 4 + y_at(d), s)

    def pos_dev(p):
        return (p * 4 + y, s)

    def owner(t):
        zt = t % 8
        return zt * 2 + (t + t // 8 + core) % 2

    has_low = (z + core) % 2 == xl
    own_tile = jnp.where(has_low, z, 8)
    owns = has_low | (z == 0)

    up_dev = ((layer + 1) % nl, s)
    dn_dev = ((layer + nl - 1) % nl, s)

    def remote(src, dst, ss, rsem, dev):
        return pltpu.make_async_remote_copy(
            src_ref=src, dst_ref=dst, send_sem=ss, recv_sem=rsem, device_id=dev, device_id_type=MESH
        )

    my_half = pl.multiple_of((y % 2) * HALF, 128)
    loads = [
        pltpu.make_async_copy(prof_hbm, profv, loc.at[0]),
        pltpu.make_async_copy(res_hbm, resv, loc.at[1]),
        pltpu.make_async_copy(panel_hbm.at[0], pan, loc.at[2]),
        pltpu.make_async_copy(trans_hbm.at[0], tv, loc.at[3]),
        pltpu.make_async_copy(mass_hbm, md.at[0, pl.ds(0, LZ)], loc.at[4]),
        pltpu.make_async_copy(damp_hbm, md.at[1, pl.ds(0, LZ)], loc.at[5]),
        pltpu.make_async_copy(trans_hbm.at[0, :, pl.ds(my_half, HALF)], ty.at[y, 0], loc.at[6]),
        pltpu.make_async_copy(trans_hbm.at[0, :, pl.ds(NX + my_half, HALF)], ty.at[y, 1], loc.at[7]),
    ]
    for c in loads:
        c.start()

    barrier = pltpu.get_barrier_semaphore()
    greet = [shot_dev(k) for k in (1, 2, 3)] + [y_dev(d) for d in (1, 2, 3)]
    greet += [up_dev, dn_dev]
    greet += [pos_dev((pos + d) % NPOS) for d in range(1, NPOS)]
    for dev in greet:
        pl.semaphore_signal(barrier, inc=1, device_id=dev, device_id_type=MESH)

    first = layer * LZ

    def forcing(p):
        for shot in range(2):
            here = plane_ref[shot] == first + p
            for half in range(2):
                cols = pl.ds(half * NX, NX)
                f = resv[shot, p, :, cols].astype(F32)
                fa[0, p, shot, :, cols] = jnp.where(here, f + va[0, pl.ds(shot * NY, NY), cols], f).astype(BF16)

    loads[0].wait()
    for shot in range(2):
        for half in range(2):
            cols = pl.ds(half * NX, NX)
            va[0, pl.ds(shot * NY, NY), cols] = rolled(profv[shot, :, cols].astype(F32), shift_ref[shot])
    loads[1].wait()
    forcing(2)
    pl.semaphore_wait(barrier, len(greet))

    def f_partner(p, shot=None):
        if shot is None:
            return remote(fa.at[0, p], fa.at[2, p], f_s.at[p, 1, 0], f_r.at[p, 1, 0], shot_dev(2))
        return remote(fa.at[0, p, shot], fa.at[2, p, shot], f_s.at[p, 1, shot], f_r.at[p, 1, shot], shot_dev(2))

    def f_sibling(p):
        return remote(fa.at[0, p], fa.at[1, p], f_s.at[p, 0, 0], f_r.at[p, 0, 0], shot_dev(1))

    def f_forward(p, shot=None):
        if shot is None:
            return remote(fa.at[2, p], fa.at[3, p], f_s.at[p, 2, 0], f_r.at[p, 2, 0], shot_dev(1))
        return remote(fa.at[2, p, shot], fa.at[3, p, shot], f_s.at[p, 2, shot], f_r.at[p, 2, shot], shot_dev(1))

    def r_back(p, k, shot=None):
        if shot is None:
            return remote(rs.at[k, p], rr.at[p, s], r_s.at[p, k - 1, 0], r_r.at[p, k - 1, 0], shot_dev(k))
        return remote(
            rs.at[k, p, shot], rr.at[p, s, shot], r_s.at[p, k - 1, shot], r_r.at[p, k - 1, shot], shot_dev(k)
        )

    order = (2, 0, 1)
    for shot in range(2):
        f_partner(2, shot).start()
    f_sibling(2).start()

    def t_send(d):
        off = pl.multiple_of((y_at(d) % 2) * HALF, 128)
        return [
            remote(trans_hbm.at[0, :, pl.ds(off + part * NX, HALF)], ty.at[y, part],
                   ty_s.at[d - 1, part], ty_r.at[d - 1, part], y_dev(d))
            for part in range(2)
        ]

    t_sends = [c for d in (1, 2, 3) for c in t_send(d)]
    for c in t_sends:
        c.start()
    for p in (0, 1):
        forcing(p)
        f_sibling(p).start()

    def product(slot, planes, shot=None):
        lhs = fa[slot, planes] if shot is None else fa[slot, planes, shot]
        shape = lhs.shape[:-1] + (COLS,)
        out = jnp.dot(lhs.reshape(-1, W), pan[...], preferred_element_type=F32).astype(BF16)
        return out.reshape(shape)

    loads[2].wait()
    own = product(0, slice(0, LZ))
    for p in range(LZ):
        rr[p, s] = own[p]
    for p in order:
        f_sibling(p).wait_recv()
    sib = product(1, slice(0, LZ))
    for p in order:
        rs[1, p] = sib[p]
        r_back(p, 1).start()

    def exchange(p, shot=None):
        f_partner(p, shot).wait_recv()
        f_forward(p, shot).start()
        where = (p,) if shot is None else (p, shot)
        rs[(2,) + where] = product(2, p, shot)
        r_back(p, 2, shot).start()

    def exchange_far(p, shot=None):
        f_forward(p, shot).wait_recv()
        where = (p,) if shot is None else (p, shot)
        rs[(3,) + where] = product(3, p, shot)
        r_back(p, 3, shot).start()

    exchange(2, 0)
    exchange_far(2, 0)
    exchange(2, 1)
    f_partner(0).start()
    exchange_far(2, 1)

    loads[4].wait()
    loads[5].wait()

    def coefficients(p):
        sh = 1.0 + md[0, p].astype(F32)
        dm = md[1, p].astype(F32)
        w = RELAX / (sh * sh + dm * dm)
        coef[p, 0] = w * sh
        coef[p, 1] = -(w * dm)

    loads[3].wait()
    loads[6].wait()
    loads[7].wait()
    for c in t_sends:
        c.wait_recv()
    tr, ti = ty[0, 0], ty[0, 1]
    for j in range(1, 4):
        tr, ti = cmul(ty[j, 0], ty[j, 1], tr, ti)
    tblk[0] = tr
    tblk[1] = ti
    for t in range(NT):
        rt, ct = pl.ds((t // 3) * 16, 16), pl.ds((t % 3) * 128, 128)
        for part in range(2):
            ttile[t, part] = tblk[part, rt, ct]

    def tile_send(t, src, dst, ss, rsem):
        @pl.when(owner(t) != pos)
        def _():
            remote(src.at[t], dst.at[pos], ss.at[t], rsem.at[pos], pos_dev(owner(t))).start()

        @pl.when(owner(t) == pos)
        def _():
            dst[pos] = src[t]

    def tile_sent(t, src, dst, ss, rsem):
        @pl.when(owner(t) != pos)
        def _():
            remote(src.at[t], dst.at[pos], ss.at[t], rsem.at[pos], pos_dev(owner(t))).wait_send()

    def tile_recv(src, dst, ss, rsem):
        for q in range(NPOS):
            @pl.when(pos != q)
            def _():
                remote(src.at[0], dst.at[q], ss.at[0], rsem.at[q], pos_dev(q)).wait_recv()

    for t in range(NT):
        tile_send(t, ttile, ot, tt_s, tt_r)

    def field(p, shot, part):
        f = fa[0, p, shot, :, pl.ds(part * NX, NX)].astype(F32)
        prod = jnp.concatenate([rr[p, part * 2, shot], rr[p, part * 2 + 1, shot]], axis=-1)
        return f + prod.astype(F32)

    def b_send(i):
        return remote(bq.at[i], by.at[y], by_s.at[i], by_r.at[y], ((layer // 4) * 4 + i, s))

    def on_others(n, mine, action):
        for i in range(n):
            @pl.when(mine != i)
            def _(i=i):
                action(i)

    for shot in range(2):
        rows = pl.ds(shot * NY, NY)
        if shot == 0:
            r_back(2, 1).wait_recv()
        for k in (2, 3):
            r_back(2, k, shot).wait_recv()
        re, im = field(2, shot, 0), field(2, shot, 1)
        pf2[rows, pl.ds(0, NX)] = re
        pf2[rows, pl.ds(NX, NX)] = im
        for c in range(2):
            i = shot * 2 + c
            cut = slice(c * HALF, (c + 1) * HALF)
            bq[i, :, pl.ds(0, HALF)] = re[:, cut].astype(BF16)
            bq[i, :, pl.ds(HALF, HALF)] = im[:, cut].astype(BF16)

            @pl.when(y != i)
            def _(i=i):
                b_send(i).start()

    by[y] = bq[y]

    def local_iterate(p, slot):
        for shot in range(2):
            rows = pl.ds(shot * NY, NY)
            if p == 2:
                re, im = pf2[rows, pl.ds(0, NX)], pf2[rows, pl.ds(NX, NX)]
            else:
                re, im = field(p, shot, 0), field(p, shot, 1)
            vr, vi = cmul(coef[p, 0], coef[p, 1], re, im)
            va[p + 1, rows, pl.ds(0, NX)] = vr
            va[p + 1, rows, pl.ds(NX, NX)] = vi
            if slot is not None:
                hs[slot, rows, pl.ds(0, NX)] = vr.astype(BF16)
                hs[slot, rows, pl.ds(NX, NX)] = vi.astype(BF16)

    for p in range(LZ):
        coefficients(p)
    local_iterate(2, 0)
    halo_down = remote(hs.at[0], hr.at[0], h_s.at[0], h_r.at[0], up_dev)
    halo_up = remote(hs.at[1], hr.at[1], h_s.at[1], h_r.at[1], dn_dev)

    on_others(4, y, lambda i: remote(bq.at[0], by.at[i], by_s.at[0], by_r.at[i], y_dev(1)).wait_recv())
    re, im = by[0, :, pl.ds(0, HALF)].astype(F32), by[0, :, pl.ds(HALF, HALF)].astype(F32)
    for j in range(1, 4):
        re, im = cmul(ty[j, 0], ty[j, 1], re, im)
        re = re + by[j, :, pl.ds(0, HALF)].astype(F32)
        im = im + by[j, :, pl.ds(HALF, HALF)].astype(F32)
    for t in range(NT):
        rt, ct = slice((t // 3) * 16, (t // 3) * 16 + 16), slice((t % 3) * 128, (t % 3) * 128 + 128)
        tot[t, 0] = re[rt, ct].astype(TT)
        tot[t, 1] = im[rt, ct].astype(TT)
    for t in range(NT):
        tile_send(t, tot, ob, tot_s, tot_r)

    exchange(0)
    f_partner(1).start()
    exchange_far(0)

    def back(q):
        return remote(ibs.at[q], inb.at[own_tile], ib_s.at[q], ib_r.at[own_tile], pos_dev(q))

    @pl.when(owns)
    def _():
        tile_recv(ttile, ot, tt_s, tt_r)
        tile_recv(tot, ob, tot_s, tot_r)
        cr = jnp.zeros((16, 128), F32)
        ci = jnp.zeros((16, 128), F32)
        for q in range(NPOS):
            ibs[q, 0] = cr.astype(TT)
            ibs[q, 1] = ci.astype(TT)

            @pl.when(pos != q)
            def _():
                back(q).start()

            if q < NPOS - 1:
                cr, ci = cmul(ot[q, 0], ot[q, 1], cr, ci)
                cr = cr + ob[q, 0].astype(F32)
                ci = ci + ob[q, 1].astype(F32)
        inb[own_tile] = ibs[pos]

    exchange(1)
    exchange_far(1)
    for k in (1, 2, 3):
        r_back(0, k).wait_recv()
    local_iterate(0, 1)
    halo_down.start()
    halo_up.start()

    def md_send(c):
        return remote((mass_hbm, damp_hbm)[c].at[0], md.at[c, LZ], md_s.at[0], md_r.at[0], dn_dev)

    def md_forward(c):
        return remote(md.at[c, LZ], md.at[c, LZ], md_s.at[1], md_r.at[1], shot_dev(1))

    def by_core(action):
        for c in range(2):
            @pl.when(core == c)
            def _(c=c):
                action(c)

    by_core(lambda c: md_send(c).start())

    for t in range(NT):
        @pl.when(owner(t) != pos)
        def _():
            remote(ibs.at[0], inb.at[t], ib_s.at[0], ib_r.at[t], pos_dev(owner(t))).wait_recv()
    parts = [
        jnp.concatenate(
            [jnp.concatenate([inb[rt * 3 + ct, part] for ct in range(3)], axis=-1) for rt in range(3)], axis=0
        ).astype(F32)
        for part in range(2)
    ]
    re, im = parts
    for j in range(4):
        ins[j, :, pl.ds(0, HALF)] = re.astype(BF16)
        ins[j, :, pl.ds(HALF, HALF)] = im.astype(BF16)
        if j < 3:
            re, im = cmul(ty[j, 0], ty[j, 1], re, im)
            re = re + by[j, :, pl.ds(0, HALF)].astype(F32)
            im = im + by[j, :, pl.ds(HALF, HALF)].astype(F32)

    def in_send(d):
        return remote(ins.at[y_at(d)], inc.at[y], in_s.at[d - 1], in_r.at[d - 1], y_dev(d))

    for d in (1, 2, 3):
        in_send(d).start()
    inc[y] = ins[y]

    for k in (1, 2, 3):
        r_back(1, k).wait_recv()
    local_iterate(1, None)

    md_send(0).wait_recv()
    by_core(lambda c: md_forward(c).start())
    halo_down.wait_recv()
    halo_up.wait_recv()
    md_forward(0).wait_recv()
    coefficients(LZ)
    not_first = jnp.where(layer == 0, 0.0, 1.0).astype(F32)
    not_last = jnp.where(layer == nl - 1, 0.0, 1.0).astype(F32)
    va[0] = hr[0].astype(F32) * not_first

    for d in (1, 2, 3):
        in_send(d).wait_recv()
    for shot in range(2):
        rows = pl.ds(shot * NY, NY)
        re = jnp.concatenate([inc[shot * 2 + c, :, pl.ds(0, HALF)] for c in range(2)], axis=-1).astype(F32)
        im = jnp.concatenate([inc[shot * 2 + c, :, pl.ds(HALF, HALF)] for c in range(2)], axis=-1).astype(F32)
        vr, vi = cmul(coef[0, 0], coef[0, 1], re, im)
        rcols, icols = pl.ds(0, NX), pl.ds(NX, NX)
        va[1, rows, rcols] += vr
        va[1, rows, icols] += vi
        nr, ni = cmul(tv[:, rcols], tv[:, icols], re, im)
        nr = nr + pf2[rows, rcols]
        ni = ni + pf2[rows, icols]
        vr, vi = cmul(coef[LZ, 0], coef[LZ, 1], nr, ni)
        va[4, rows, rcols] = (vr + hr[1, rows, rcols].astype(F32)) * not_last
        va[4, rows, icols] = (vi + hr[1, rows, icols].astype(F32)) * not_last

    outs = []
    for p in range(LZ):
        for shot in range(2):
            rows = pl.ds(shot * NY, NY)
            diff = []
            for part in range(2):
                cols = pl.ds(part * NX, NX)
                mid = va[p + 1, rows, cols]
                w = mid + 0.5 * (va[p, rows, cols] + va[p + 2, rows, cols])
                diff.append(lateral(w) - mid)
            dr, di = cmul(coef[p, 0], coef[p, 1], diff[0], diff[1])
            outv[shot, p, :, pl.ds(0, NX)] = (1.2 * va[p + 1, rows, pl.ds(0, NX)] + dr * (1.0 / 7.0)).astype(BF16)
            outv[shot, p, :, pl.ds(NX, NX)] = (1.2 * va[p + 1, rows, pl.ds(NX, NX)] + di * (1.0 / 7.0)).astype(BF16)
            c = pltpu.make_async_copy(outv.at[shot, p], out_hbm.at[shot, p], out_s.at[shot, p])
            c.start()
            outs.append(c)

    for shot in range(2):
        f_partner(2, shot).wait_send()
        f_forward(2, shot).wait_send()
        for k in (2, 3):
            r_back(2, k, shot).wait_send()
    for p in (0, 1):
        f_partner(p).wait_send()
        f_forward(p).wait_send()
        for k in (2, 3):
            r_back(p, k).wait_send()
    for p in order:
        f_sibling(p).wait_send()
        r_back(p, 1).wait_send()
    for c in t_sends + [halo_down, halo_up, md_send(0), md_forward(0)]:
        c.wait_send()
    on_others(4, y, lambda i: b_send(i).wait_send())
    for d in (1, 2, 3):
        in_send(d).wait_send()
    for t in range(NT):
        tile_sent(t, ttile, ot, tt_s, tt_r)
        tile_sent(t, tot, ob, tot_s, tot_r)

    @pl.when(owns)
    def _():
        for q in range(NPOS):
            @pl.when(pos != q)
            def _():
                back(q).wait_send()

    for c in outs:
        c.wait()


def on_device(residual_src, src_plane, src_shift, profile, mass, damping, panel, transmission):
    smem = pl.BlockSpec(memory_space=pltpu.SMEM)
    hbm = pl.BlockSpec(memory_space=pl.ANY)
    dma = pltpu.SemaphoreType.DMA
    scratch = [
        pltpu.VMEM((2, LZ, NY, W), BF16),
        pltpu.VMEM((2, NY, W), BF16),
        pltpu.VMEM((W, COLS), BF16),
        pltpu.VMEM((4, LZ, 2, NY, W), BF16),
        pltpu.VMEM((4, LZ, 2, NY, COLS), BF16),
        pltpu.VMEM((LZ, 4, 2, NY, COLS), BF16),
        pltpu.VMEM((2, LZ + 1, NY, NX), BF16),
        pltpu.VMEM((LZ + 1, 2, NY, NX), F32),
        pltpu.VMEM((NY, W), F32),
        pltpu.VMEM((4, 2, NY, HALF), F32),
        pltpu.VMEM((2, NY, HALF), F32),
        pltpu.VMEM((NT, 2, 16, 128), F32),
        pltpu.VMEM((NPOS, 2, 16, 128), F32),
        pltpu.VMEM((ROWS, W), F32),
        pltpu.VMEM((4, NY, NX), BF16),
        pltpu.VMEM((4, NY, NX), BF16),
        pltpu.VMEM((NT, 2, 16, 128), TT),
        pltpu.VMEM((NPOS, 2, 16, 128), TT),
        pltpu.VMEM((NPOS, 2, 16, 128), TT),
        pltpu.VMEM((NT, 2, 16, 128), TT),
        pltpu.VMEM((4, NY, NX), BF16),
        pltpu.VMEM((4, NY, NX), BF16),
        pltpu.VMEM((5, ROWS, W), F32),
        pltpu.VMEM((2, ROWS, W), BF16),
        pltpu.VMEM((2, ROWS, W), BF16),
        pltpu.VMEM((2, LZ, NY, W), BF16),
        dma((8,)), dma((LZ, 3, 2)), dma((LZ, 3, 2)), dma((LZ, 3, 2)), dma((LZ, 3, 2)), dma((2,)), dma((2,)),
        dma((3, 2)), dma((3, 2)), dma((NT,)), dma((NPOS,)),
        dma((4,)), dma((4,)), dma((NT,)), dma((NPOS,)), dma((NPOS,)), dma((NT,)),
        dma((3,)), dma((3,)), dma((2,)), dma((2,)), dma((2, LZ)),
    ]
    return pl.pallas_call(
        sweep_kernel,
        out_shape=jax.ShapeDtypeStruct((2, LZ, NY, W), BF16),
        in_specs=[smem] * 2 + [hbm] * 6,
        out_specs=hbm,
        scratch_shapes=scratch,
        name="sweep",
        compiler_params=pltpu.CompilerParams(
            collective_id=0, has_side_effects=True, vmem_limit_bytes=56 * 2**20
        ),
    )(src_plane, src_shift, residual_src, profile, mass, damping, panel, transmission)


def solution(mesh):
    placed = (
        P("shot", "layer", None, None),
        P("shot"),
        P("shot"),
        P("shot", None, None),
        P("layer", None, None),
        P("layer", None, None),
        P("layer", None, "shot"),
        P("layer", None, None),
    )
    return jax.shard_map(
        on_device,
        mesh=mesh,
        in_specs=placed,
        out_specs=P("shot", "layer", None, None),
        check_vma=False,
    )
```

```python
import jax
import jax.numpy as jnp
from jax import lax
from jax.experimental import pallas as pl
from jax.experimental.pallas import tpu as pltpu
from jax.sharding import PartitionSpec as P

MESH = pl.DeviceIdType.MESH
F32, BF16 = jnp.float32, jnp.bfloat16
RELAX = 0.8
TT = BF16
NY, NX, W, LZ = 48, 768, 1536, 3
ROWS = 2 * NY
COLS = 384
HALF = 384
NT = 9
NPOS = 16


def rolled(x, shift):
    for k in range(10):
        x = jnp.where((shift >> k) & 1 == 1, pltpu.roll(x, 1 << k, axis=1), x)
    return x


def cmul(ar, ai, br, bi):
    return ar * br - ai * bi, ar * bi + ai * br


def lateral(w):
    col = lax.broadcasted_iota(jnp.int32, w.shape, 1)
    row = lax.broadcasted_iota(jnp.int32, w.shape, 0)
    left = jnp.where(col == 0, 0.0, pltpu.roll(w, 1, axis=1))
    right = jnp.where(col == w.shape[1] - 1, 0.0, pltpu.roll(w, w.shape[1] - 1, axis=1))
    w = w + 0.5 * (left + right)
    up = jnp.where(row == 0, 0.0, pltpu.roll(w, 1, axis=0))
    down = jnp.where(row == w.shape[0] - 1, 0.0, pltpu.roll(w, w.shape[0] - 1, axis=0))
    return w + 0.5 * (up + down)


def sweep_kernel(
    plane_ref, shift_ref, res_hbm, prof_hbm, mass_hbm, damp_hbm, panel_hbm, trans_hbm, out_hbm,
    resv, profv, pan, fa, rs, rr, md, coef, tv, ty, tblk, ttile, ot,
    pf2, bq, by, tot, ob, ibs, inb, ins, inc, va, hs, hr, outv,
    loc, f_s, f_r, r_s, r_r, md_s, md_r, ty_s, ty_r, tt_s, tt_r,
    by_s, by_r, tot_s, tot_r, ib_s, ib_r, in_s, in_r, h_s, h_r, out_s,
):
    layer, s = lax.axis_index("layer"), lax.axis_index("shot")
    nl = 64
    z, xl, y = layer // 8, (layer // 4) % 2, layer % 4
    xh, core = s // 2, s % 2
    pos = layer // 4

    def rel(k):
        c = (core + k % 2) % 2
        x = (xh + k // 2) % 2
        return x * 2 + c

    def shot_dev(k):
        return (layer, rel(k))

    def y_at(d):
        return (y + d) % 4

    def y_dev(d):
        return ((layer // 4) * 4 + y_at(d), s)

    def pos_dev(p):
        return (p * 4 + y, s)

    def owner(t):
        zt = t % 8
        return zt * 2 + (t + t // 8 + core) % 2

    has_low = (z + core) % 2 == xl
    own_tile = jnp.where(has_low, z, 8)
    owns = has_low | (z == 0)

    up_dev = ((layer + 1) % nl, s)
    dn_dev = ((layer + nl - 1) % nl, s)

    def remote(src, dst, ss, rsem, dev):
        return pltpu.make_async_remote_copy(
            src_ref=src, dst_ref=dst, send_sem=ss, recv_sem=rsem, device_id=dev, device_id_type=MESH
        )

    my_half = pl.multiple_of((y % 2) * HALF, 128)
    loads = [
        pltpu.make_async_copy(prof_hbm, profv, loc.at[0]),
        pltpu.make_async_copy(res_hbm, resv, loc.at[1]),
        pltpu.make_async_copy(panel_hbm.at[0], pan, loc.at[2]),
        pltpu.make_async_copy(trans_hbm.at[0], tv, loc.at[3]),
        pltpu.make_async_copy(mass_hbm, md.at[0, pl.ds(0, LZ)], loc.at[4]),
        pltpu.make_async_copy(damp_hbm, md.at[1, pl.ds(0, LZ)], loc.at[5]),
        pltpu.make_async_copy(trans_hbm.at[0, :, pl.ds(my_half, HALF)], ty.at[y, 0], loc.at[6]),
        pltpu.make_async_copy(trans_hbm.at[0, :, pl.ds(NX + my_half, HALF)], ty.at[y, 1], loc.at[7]),
    ]
    for c in loads:
        c.start()

    barrier = pltpu.get_barrier_semaphore()
    greet = [shot_dev(k) for k in (1, 2, 3)] + [y_dev(d) for d in (1, 2, 3)]
    greet += [up_dev, dn_dev]
    greet += [pos_dev((pos + d) % NPOS) for d in range(1, NPOS)]
    for dev in greet:
        pl.semaphore_signal(barrier, inc=1, device_id=dev, device_id_type=MESH)

    first = layer * LZ

    def forcing(p):
        for shot in range(2):
            here = plane_ref[shot] == first + p
            for half in range(2):
                cols = pl.ds(half * NX, NX)
                f = resv[shot, p, :, cols].astype(F32)
                fa[0, p, shot, :, cols] = jnp.where(here, f + va[0, pl.ds(shot * NY, NY), cols], f).astype(BF16)

    loads[0].wait()
    for shot in range(2):
        for half in range(2):
            cols = pl.ds(half * NX, NX)
            va[0, pl.ds(shot * NY, NY), cols] = rolled(profv[shot, :, cols].astype(F32), shift_ref[shot])
    loads[1].wait()
    forcing(2)
    pl.semaphore_wait(barrier, len(greet))

    def f_partner(p, shot):
        return remote(fa.at[0, p, shot], fa.at[2, p, shot], f_s.at[p, 1, shot], f_r.at[p, 1, shot], shot_dev(2))

    def f_sibling(p):
        return remote(fa.at[0, p], fa.at[1, p], f_s.at[p, 0, 0], f_r.at[p, 0, 0], shot_dev(1))

    def f_forward(p, shot):
        return remote(fa.at[2, p, shot], fa.at[3, p, shot], f_s.at[p, 2, shot], f_r.at[p, 2, shot], shot_dev(1))

    def r_back(p, k, shot=None):
        if shot is None:
            return remote(rs.at[k, p], rr.at[p, s], r_s.at[p, k - 1, 0], r_r.at[p, k - 1, 0], shot_dev(k))
        return remote(
            rs.at[k, p, shot], rr.at[p, s, shot], r_s.at[p, k - 1, shot], r_r.at[p, k - 1, shot], shot_dev(k)
        )

    order = (2, 0, 1)
    for shot in range(2):
        f_partner(2, shot).start()
    f_sibling(2).start()

    def t_send(d):
        off = pl.multiple_of((y_at(d) % 2) * HALF, 128)
        return [
            remote(trans_hbm.at[0, :, pl.ds(off + part * NX, HALF)], ty.at[y, part],
                   ty_s.at[d - 1, part], ty_r.at[d - 1, part], y_dev(d))
            for part in range(2)
        ]

    t_sends = [c for d in (1, 2, 3) for c in t_send(d)]
    for c in t_sends:
        c.start()
    for p in (0, 1):
        forcing(p)
        f_sibling(p).start()

    def product(slot, planes, shot=None):
        lhs = fa[slot, planes] if shot is None else fa[slot, planes, shot]
        shape = lhs.shape[:-1] + (COLS,)
        out = jnp.dot(lhs.reshape(-1, W), pan[...], preferred_element_type=F32).astype(BF16)
        return out.reshape(shape)

    loads[2].wait()
    own = product(0, slice(0, LZ))
    for p in range(LZ):
        rr[p, s] = own[p]
    for p in order:
        f_sibling(p).wait_recv()
    sib = product(1, slice(0, LZ))
    for p in order:
        rs[1, p] = sib[p]
        r_back(p, 1).start()

    pieces = [(p, shot) for p in order for shot in range(2)]

    def step(n):
        p, shot = pieces[n]
        f_partner(p, shot).wait_recv()
        f_forward(p, shot).start()
        if n + 2 < len(pieces):
            f_partner(*pieces[n + 2]).start()
        rs[2, p, shot] = product(2, p, shot)
        r_back(p, 2, shot).start()
        f_forward(p, shot).wait_recv()
        rs[3, p, shot] = product(3, p, shot)
        r_back(p, 3, shot).start()

    step(0)
    step(1)

    def md_send(c):
        return remote((mass_hbm, damp_hbm)[c].at[0], md.at[c, LZ], md_s.at[0], md_r.at[0], dn_dev)

    def md_forward(c):
        return remote(md.at[c, LZ], md.at[c, LZ], md_s.at[1], md_r.at[1], shot_dev(1))

    def by_core(action):
        for c in range(2):
            @pl.when(core == c)
            def _(c=c):
                action(c)

    by_core(lambda c: md_send(c).start())

    loads[4].wait()
    loads[5].wait()

    def coefficients(p):
        sh = 1.0 + md[0, p].astype(F32)
        dm = md[1, p].astype(F32)
        w = RELAX / (sh * sh + dm * dm)
        coef[p, 0] = w * sh
        coef[p, 1] = -(w * dm)

    loads[3].wait()
    loads[6].wait()
    loads[7].wait()
    for c in t_sends:
        c.wait_recv()
    tr, ti = ty[0, 0], ty[0, 1]
    for j in range(1, 4):
        tr, ti = cmul(ty[j, 0], ty[j, 1], tr, ti)
    tblk[0] = tr
    tblk[1] = ti
    for t in range(NT):
        rt, ct = pl.ds((t // 3) * 16, 16), pl.ds((t % 3) * 128, 128)
        for part in range(2):
            ttile[t, part] = tblk[part, rt, ct]

    def tile_send(t, src, dst, ss, rsem):
        @pl.when(owner(t) != pos)
        def _():
            remote(src.at[t], dst.at[pos], ss.at[t], rsem.at[pos], pos_dev(owner(t))).start()

        @pl.when(owner(t) == pos)
        def _():
            dst[pos] = src[t]

    def tile_sent(t, src, dst, ss, rsem):
        @pl.when(owner(t) != pos)
        def _():
            remote(src.at[t], dst.at[pos], ss.at[t], rsem.at[pos], pos_dev(owner(t))).wait_send()

    def tile_recv(src, dst, ss, rsem):
        for q in range(NPOS):
            @pl.when(pos != q)
            def _():
                remote(src.at[0], dst.at[q], ss.at[0], rsem.at[q], pos_dev(q)).wait_recv()

    for t in range(NT):
        tile_send(t, ttile, ot, tt_s, tt_r)

    def field(p, shot, part):
        f = fa[0, p, shot, :, pl.ds(part * NX, NX)].astype(F32)
        prod = jnp.concatenate([rr[p, part * 2, shot], rr[p, part * 2 + 1, shot]], axis=-1)
        return f + prod.astype(F32)

    def b_send(i):
        return remote(bq.at[i], by.at[y], by_s.at[i], by_r.at[y], ((layer // 4) * 4 + i, s))

    def on_others(n, mine, action):
        for i in range(n):
            @pl.when(mine != i)
            def _(i=i):
                action(i)

    for shot in range(2):
        rows = pl.ds(shot * NY, NY)
        if shot == 0:
            r_back(2, 1).wait_recv()
        for k in (2, 3):
            r_back(2, k, shot).wait_recv()
        re, im = field(2, shot, 0), field(2, shot, 1)
        pf2[rows, pl.ds(0, NX)] = re
        pf2[rows, pl.ds(NX, NX)] = im
        for c in range(2):
            i = shot * 2 + c
            cut = slice(c * HALF, (c + 1) * HALF)
            bq[i, :, pl.ds(0, HALF)] = re[:, cut].astype(BF16)
            bq[i, :, pl.ds(HALF, HALF)] = im[:, cut].astype(BF16)

            @pl.when(y != i)
            def _(i=i):
                b_send(i).start()

    by[y] = bq[y]

    def local_iterate(p, slot):
        for shot in range(2):
            rows = pl.ds(shot * NY, NY)
            if p == 2:
                re, im = pf2[rows, pl.ds(0, NX)], pf2[rows, pl.ds(NX, NX)]
            else:
                re, im = field(p, shot, 0), field(p, shot, 1)
            vr, vi = cmul(coef[p, 0], coef[p, 1], re, im)
            va[p + 1, rows, pl.ds(0, NX)] = vr
            va[p + 1, rows, pl.ds(NX, NX)] = vi
            if slot is not None:
                hs[slot, rows, pl.ds(0, NX)] = vr.astype(BF16)
                hs[slot, rows, pl.ds(NX, NX)] = vi.astype(BF16)

    for p in range(LZ):
        coefficients(p)
    local_iterate(2, 0)
    halo_down = remote(hs.at[0], hr.at[0], h_s.at[0], h_r.at[0], up_dev)
    halo_up = remote(hs.at[1], hr.at[1], h_s.at[1], h_r.at[1], dn_dev)

    step(2)

    on_others(4, y, lambda i: remote(bq.at[0], by.at[i], by_s.at[0], by_r.at[i], y_dev(1)).wait_recv())
    re, im = by[0, :, pl.ds(0, HALF)].astype(F32), by[0, :, pl.ds(HALF, HALF)].astype(F32)
    for j in range(1, 4):
        re, im = cmul(ty[j, 0], ty[j, 1], re, im)
        re = re + by[j, :, pl.ds(0, HALF)].astype(F32)
        im = im + by[j, :, pl.ds(HALF, HALF)].astype(F32)
    for t in range(NT):
        rt, ct = slice((t // 3) * 16, (t // 3) * 16 + 16), slice((t % 3) * 128, (t % 3) * 128 + 128)
        tot[t, 0] = re[rt, ct].astype(TT)
        tot[t, 1] = im[rt, ct].astype(TT)
    for t in range(NT):
        tile_send(t, tot, ob, tot_s, tot_r)

    step(3)

    def back(q):
        return remote(ibs.at[q], inb.at[own_tile], ib_s.at[q], ib_r.at[own_tile], pos_dev(q))

    @pl.when(owns)
    def _():
        tile_recv(ttile, ot, tt_s, tt_r)
        tile_recv(tot, ob, tot_s, tot_r)
        cr = jnp.zeros((16, 128), F32)
        ci = jnp.zeros((16, 128), F32)
        for q in range(NPOS):
            ibs[q, 0] = cr.astype(TT)
            ibs[q, 1] = ci.astype(TT)

            @pl.when(pos != q)
            def _():
                back(q).start()

            if q < NPOS - 1:
                cr, ci = cmul(ot[q, 0], ot[q, 1], cr, ci)
                cr = cr + ob[q, 0].astype(F32)
                ci = ci + ob[q, 1].astype(F32)
        inb[own_tile] = ibs[pos]

    md_send(0).wait_recv()
    by_core(lambda c: md_forward(c).start())
    step(4)
    md_forward(0).wait_recv()
    coefficients(LZ)

    def products_in(p):
        r_back(p, 1).wait_recv()
        for shot in range(2):
            for k in (2, 3):
                r_back(p, k, shot).wait_recv()

    products_in(0)
    local_iterate(0, 1)

    for t in range(NT):
        @pl.when(owner(t) != pos)
        def _():
            remote(ibs.at[0], inb.at[t], ib_s.at[0], ib_r.at[t], pos_dev(owner(t))).wait_recv()
    parts = [
        jnp.concatenate(
            [jnp.concatenate([inb[rt * 3 + ct, part] for ct in range(3)], axis=-1) for rt in range(3)], axis=0
        ).astype(F32)
        for part in range(2)
    ]
    re, im = parts
    for j in range(4):
        ins[j, :, pl.ds(0, HALF)] = re.astype(BF16)
        ins[j, :, pl.ds(HALF, HALF)] = im.astype(BF16)
        if j < 3:
            re, im = cmul(ty[j, 0], ty[j, 1], re, im)
            re = re + by[j, :, pl.ds(0, HALF)].astype(F32)
            im = im + by[j, :, pl.ds(HALF, HALF)].astype(F32)

    def in_send(d):
        return remote(ins.at[y_at(d)], inc.at[y], in_s.at[d - 1], in_r.at[d - 1], y_dev(d))

    for d in (1, 2, 3):
        in_send(d).start()
    inc[y] = ins[y]

    step(5)
    halo_down.start()
    halo_up.start()

    products_in(1)
    local_iterate(1, None)

    not_first = jnp.where(layer == 0, 0.0, 1.0).astype(F32)
    not_last = jnp.where(layer == nl - 1, 0.0, 1.0).astype(F32)
    rcols, icols = pl.ds(0, NX), pl.ds(NX, NX)

    for d in (1, 2, 3):
        in_send(d).wait_recv()
    for shot in range(2):
        rows = pl.ds(shot * NY, NY)
        re = jnp.concatenate([inc[shot * 2 + c, :, pl.ds(0, HALF)] for c in range(2)], axis=-1).astype(F32)
        im = jnp.concatenate([inc[shot * 2 + c, :, pl.ds(HALF, HALF)] for c in range(2)], axis=-1).astype(F32)
        vr, vi = cmul(coef[0, 0], coef[0, 1], re, im)
        va[1, rows, rcols] += vr
        va[1, rows, icols] += vi
        nr, ni = cmul(tv[:, rcols], tv[:, icols], re, im)
        nr = nr + pf2[rows, rcols]
        ni = ni + pf2[rows, icols]
        vr, vi = cmul(coef[LZ, 0], coef[LZ, 1], nr, ni)
        va[4, rows, rcols] = vr
        va[4, rows, icols] = vi

    outs = []

    def finish(p):
        for shot in range(2):
            rows = pl.ds(shot * NY, NY)
            diff = []
            for part in range(2):
                cols = pl.ds(part * NX, NX)
                mid = va[p + 1, rows, cols]
                above, below = va[p, rows, cols], va[p + 2, rows, cols]
                if p == 0:
                    above = hr[0, rows, cols].astype(F32) * not_first
                if p == LZ - 1:
                    below = (below + hr[1, rows, cols].astype(F32)) * not_last
                w = mid + 0.5 * (above + below)
                diff.append(lateral(w) - mid)
            dr, di = cmul(coef[p, 0], coef[p, 1], diff[0], diff[1])
            outv[shot, p, :, rcols] = (1.2 * va[p + 1, rows, rcols] + dr * (1.0 / 7.0)).astype(BF16)
            outv[shot, p, :, icols] = (1.2 * va[p + 1, rows, icols] + di * (1.0 / 7.0)).astype(BF16)
            c = pltpu.make_async_copy(outv.at[shot, p], out_hbm.at[shot, p], out_s.at[shot, p])
            c.start()
            outs.append(c)

    finish(1)
    halo_down.wait_recv()
    finish(0)
    halo_up.wait_recv()
    finish(2)

    for p, shot in pieces:
        f_partner(p, shot).wait_send()
        f_forward(p, shot).wait_send()
        for k in (2, 3):
            r_back(p, k, shot).wait_send()
    for p in order:
        f_sibling(p).wait_send()
        r_back(p, 1).wait_send()
    for c in t_sends + [halo_down, halo_up, md_send(0), md_forward(0)]:
        c.wait_send()
    on_others(4, y, lambda i: b_send(i).wait_send())
    for d in (1, 2, 3):
        in_send(d).wait_send()
    for t in range(NT):
        tile_sent(t, ttile, ot, tt_s, tt_r)
        tile_sent(t, tot, ob, tot_s, tot_r)

    @pl.when(owns)
    def _():
        for q in range(NPOS):
            @pl.when(pos != q)
            def _():
                back(q).wait_send()

    for c in outs:
        c.wait()


def on_device(residual_src, src_plane, src_shift, profile, mass, damping, panel, transmission):
    smem = pl.BlockSpec(memory_space=pltpu.SMEM)
    hbm = pl.BlockSpec(memory_space=pltpu.HBM)
    dma = pltpu.SemaphoreType.DMA
    scratch = [
        pltpu.VMEM((2, LZ, NY, W), BF16),
        pltpu.VMEM((2, NY, W), BF16),
        pltpu.VMEM((W, COLS), BF16),
        pltpu.VMEM((4, LZ, 2, NY, W), BF16),
        pltpu.VMEM((4, LZ, 2, NY, COLS), BF16),
        pltpu.VMEM((LZ, 4, 2, NY, COLS), BF16),
        pltpu.VMEM((2, LZ + 1, NY, NX), BF16),
        pltpu.VMEM((LZ + 1, 2, NY, NX), F32),
        pltpu.VMEM((NY, W), F32),
        pltpu.VMEM((4, 2, NY, HALF), F32),
        pltpu.VMEM((2, NY, HALF), F32),
        pltpu.VMEM((NT, 2, 16, 128), F32),
        pltpu.VMEM((NPOS, 2, 16, 128), F32),
        pltpu.VMEM((ROWS, W), F32),
        pltpu.VMEM((4, NY, NX), BF16),
        pltpu.VMEM((4, NY, NX), BF16),
        pltpu.VMEM((NT, 2, 16, 128), TT),
        pltpu.VMEM((NPOS, 2, 16, 128), TT),
        pltpu.VMEM((NPOS, 2, 16, 128), TT),
        pltpu.VMEM((NT, 2, 16, 128), TT),
        pltpu.VMEM((4, NY, NX), BF16),
        pltpu.VMEM((4, NY, NX), BF16),
        pltpu.VMEM((5, ROWS, W), F32),
        pltpu.VMEM((2, ROWS, W), BF16),
        pltpu.VMEM((2, ROWS, W), BF16),
        pltpu.VMEM((2, LZ, NY, W), BF16),
        dma((8,)), dma((LZ, 3, 2)), dma((LZ, 3, 2)), dma((LZ, 3, 2)), dma((LZ, 3, 2)), dma((2,)), dma((2,)),
        dma((3, 2)), dma((3, 2)), dma((NT,)), dma((NPOS,)),
        dma((4,)), dma((4,)), dma((NT,)), dma((NPOS,)), dma((NPOS,)), dma((NT,)),
        dma((3,)), dma((3,)), dma((2,)), dma((2,)), dma((2, LZ)),
    ]
    return pl.pallas_call(
        sweep_kernel,
        out_shape=jax.ShapeDtypeStruct((2, LZ, NY, W), BF16),
        in_specs=[smem] * 2 + [hbm] * 6,
        out_specs=pl.BlockSpec(memory_space=pl.ANY),
        scratch_shapes=scratch,
        name="sweep",
        compiler_params=pltpu.CompilerParams(
            collective_id=0, has_side_effects=True, vmem_limit_bytes=56 * 2**20
        ),
    )(src_plane, src_shift, residual_src, profile, mass, damping, panel, transmission)


def solution(mesh):
    placed = (
        P("shot", "layer", None, None),
        P("shot"),
        P("shot"),
        P("shot", None, None),
        P("layer", None, None),
        P("layer", None, None),
        P("layer", None, "shot"),
        P("layer", None, None),
    )
    return jax.shard_map(
        on_device,
        mesh=mesh,
        in_specs=placed,
        out_specs=P("shot", "layer", None, None),
        check_vma=False,
    )
```

```python
import jax
import jax.numpy as jnp
from jax import lax
from jax.experimental import pallas as pl
from jax.experimental.pallas import tpu as pltpu
from jax.sharding import PartitionSpec as P

MESH = pl.DeviceIdType.MESH
F32, BF16 = jnp.float32, jnp.bfloat16
RELAX = 0.8
ISSUE = ((), (2,), (), (), (), ())
LATE = ((), (3,), (4,), (5,), (), ())
TT = BF16
NY, NX, W, LZ = 48, 768, 1536, 3
ROWS = 2 * NY
COLS = 384
HALF = 384
NT = 9
NPOS = 16


def rolled(x, shift):
    for k in range(10):
        x = jnp.where((shift >> k) & 1 == 1, pltpu.roll(x, 1 << k, axis=1), x)
    return x


def cmul(ar, ai, br, bi):
    return ar * br - ai * bi, ar * bi + ai * br


def lateral(w):
    col = lax.broadcasted_iota(jnp.int32, w.shape, 1)
    row = lax.broadcasted_iota(jnp.int32, w.shape, 0)
    left = jnp.where(col == 0, 0.0, pltpu.roll(w, 1, axis=1))
    right = jnp.where(col == w.shape[1] - 1, 0.0, pltpu.roll(w, w.shape[1] - 1, axis=1))
    w = w + 0.5 * (left + right)
    up = jnp.where(row == 0, 0.0, pltpu.roll(w, 1, axis=0))
    down = jnp.where(row == w.shape[0] - 1, 0.0, pltpu.roll(w, w.shape[0] - 1, axis=0))
    return w + 0.5 * (up + down)


def sweep_kernel(
    plane_ref, shift_ref, res_hbm, prof_hbm, mass_hbm, damp_hbm, panel_hbm, trans_hbm, out_hbm,
    resv, profv, pan, fa, rs, rr, md, coef, tv, ty, tblk, ttile, ot,
    pf2, bq, by, tot, ob, ibs, inb, ins, inc, va, hs, hr, outv,
    loc, f_s, f_r, r_s, r_r, md_s, md_r, ty_s, ty_r, tt_s, tt_r,
    by_s, by_r, tot_s, tot_r, ib_s, ib_r, in_s, in_r, h_s, h_r, out_s,
):
    layer, s = lax.axis_index("layer"), lax.axis_index("shot")
    nl = 64
    z, xl, y = layer // 8, (layer // 4) % 2, layer % 4
    xh, core = s // 2, s % 2
    pos = layer // 4

    def rel(k):
        c = (core + k % 2) % 2
        x = (xh + k // 2) % 2
        return x * 2 + c

    def shot_dev(k):
        return (layer, rel(k))

    def y_at(d):
        return (y + d) % 4

    def y_dev(d):
        return ((layer // 4) * 4 + y_at(d), s)

    def pos_dev(p):
        return (p * 4 + y, s)

    def owner(t):
        zt = t % 8
        return zt * 2 + (t + t // 8 + core) % 2

    has_low = (z + core) % 2 == xl
    own_tile = jnp.where(has_low, z, 8)
    owns = has_low | (z == 0)

    up_dev = ((layer + 1) % nl, s)
    dn_dev = ((layer + nl - 1) % nl, s)

    def remote(src, dst, ss, rsem, dev):
        return pltpu.make_async_remote_copy(
            src_ref=src, dst_ref=dst, send_sem=ss, recv_sem=rsem, device_id=dev, device_id_type=MESH
        )

    my_half = pl.multiple_of((y % 2) * HALF, 128)
    loads = [
        pltpu.make_async_copy(prof_hbm, profv, loc.at[0]),
        pltpu.make_async_copy(res_hbm, resv, loc.at[1]),
        pltpu.make_async_copy(panel_hbm.at[0], pan, loc.at[2]),
        pltpu.make_async_copy(trans_hbm.at[0], tv, loc.at[3]),
        pltpu.make_async_copy(mass_hbm, md.at[0, pl.ds(0, LZ)], loc.at[4]),
        pltpu.make_async_copy(damp_hbm, md.at[1, pl.ds(0, LZ)], loc.at[5]),
        pltpu.make_async_copy(trans_hbm.at[0, :, pl.ds(my_half, HALF)], ty.at[y, 0], loc.at[6]),
        pltpu.make_async_copy(trans_hbm.at[0, :, pl.ds(NX + my_half, HALF)], ty.at[y, 1], loc.at[7]),
    ]
    for c in loads:
        c.start()

    barrier = pltpu.get_barrier_semaphore()
    greet = [shot_dev(k) for k in (1, 2, 3)] + [y_dev(d) for d in (1, 2, 3)]
    greet += [up_dev, dn_dev]
    greet += [pos_dev((pos + d) % NPOS) for d in range(1, NPOS)]
    for dev in greet:
        pl.semaphore_signal(barrier, inc=1, device_id=dev, device_id_type=MESH)

    first = layer * LZ

    def forcing(p):
        for shot in range(2):
            here = plane_ref[shot] == first + p
            for half in range(2):
                cols = pl.ds(half * NX, NX)
                f = resv[shot, p, :, cols].astype(F32)
                fa[0, p, shot, :, cols] = jnp.where(here, f + va[0, pl.ds(shot * NY, NY), cols], f).astype(BF16)

    loads[0].wait()
    for shot in range(2):
        for half in range(2):
            cols = pl.ds(half * NX, NX)
            va[0, pl.ds(shot * NY, NY), cols] = rolled(profv[shot, :, cols].astype(F32), shift_ref[shot])
    loads[1].wait()
    forcing(2)
    pl.semaphore_wait(barrier, len(greet))

    def f_partner(p, shot):
        return remote(fa.at[0, p, shot], fa.at[2, p, shot], f_s.at[p, 1, shot], f_r.at[p, 1, shot], shot_dev(2))

    def f_sibling(p):
        return remote(fa.at[0, p], fa.at[1, p], f_s.at[p, 0, 0], f_r.at[p, 0, 0], shot_dev(1))

    def f_forward(p, shot):
        return remote(fa.at[2, p, shot], fa.at[3, p, shot], f_s.at[p, 2, shot], f_r.at[p, 2, shot], shot_dev(1))

    def r_back(p, k, shot=None):
        if shot is None:
            return remote(rs.at[k, p], rr.at[p, s], r_s.at[p, k - 1, 0], r_r.at[p, k - 1, 0], shot_dev(k))
        return remote(
            rs.at[k, p, shot], rr.at[p, s, shot], r_s.at[p, k - 1, shot], r_r.at[p, k - 1, shot], shot_dev(k)
        )

    order = (2, 0, 1)
    for shot in range(2):
        f_partner(2, shot).start()
    f_sibling(2).start()

    def t_send(d):
        off = pl.multiple_of((y_at(d) % 2) * HALF, 128)
        return [
            remote(trans_hbm.at[0, :, pl.ds(off + part * NX, HALF)], ty.at[y, part],
                   ty_s.at[d - 1, part], ty_r.at[d - 1, part], y_dev(d))
            for part in range(2)
        ]

    t_sends = [c for d in (1, 2, 3) for c in t_send(d)]
    for c in t_sends:
        c.start()
    for p in (0, 1):
        forcing(p)
        f_sibling(p).start()

    def product(slot, planes, shot=None):
        lhs = fa[slot, planes] if shot is None else fa[slot, planes, shot]
        shape = lhs.shape[:-1] + (COLS,)
        out = jnp.dot(lhs.reshape(-1, W), pan[...], preferred_element_type=F32).astype(BF16)
        return out.reshape(shape)

    loads[2].wait()
    own = product(0, slice(0, LZ))
    for p in range(LZ):
        rr[p, s] = own[p]
    for p in order:
        f_sibling(p).wait_recv()
    sib = product(1, slice(0, LZ))
    for p in order:
        rs[1, p] = sib[p]
        r_back(p, 1).start()

    pieces = [(p, shot) for p in order for shot in range(2)]

    def step(n):
        p, shot = pieces[n]
        f_partner(p, shot).wait_recv()
        f_forward(p, shot).start()
        for m in ISSUE[n]:
            f_partner(*pieces[m]).start()
        rs[2, p, shot] = product(2, p, shot)
        r_back(p, 2, shot).start()
        f_forward(p, shot).wait_recv()
        rs[3, p, shot] = product(3, p, shot)
        r_back(p, 3, shot).start()
        for m in LATE[n]:
            f_partner(*pieces[m]).start()

    step(0)
    step(1)

    def md_send(c):
        return remote((mass_hbm, damp_hbm)[c].at[0], md.at[c, LZ], md_s.at[0], md_r.at[0], dn_dev)

    def md_forward(c):
        return remote(md.at[c, LZ], md.at[c, LZ], md_s.at[1], md_r.at[1], shot_dev(1))

    def by_core(action):
        for c in range(2):
            @pl.when(core == c)
            def _(c=c):
                action(c)

    by_core(lambda c: md_send(c).start())

    loads[4].wait()
    loads[5].wait()

    def coefficients(p):
        sh = 1.0 + md[0, p].astype(F32)
        dm = md[1, p].astype(F32)
        w = RELAX / (sh * sh + dm * dm)
        coef[p, 0] = w * sh
        coef[p, 1] = -(w * dm)

    def tile_send(t, src, dst, ss, rsem):
        @pl.when(owner(t) != pos)
        def _():
            remote(src.at[t], dst.at[pos], ss.at[t], rsem.at[pos], pos_dev(owner(t))).start()

        @pl.when(owner(t) == pos)
        def _():
            dst[pos] = src[t]

    def tile_sent(t, src, dst, ss, rsem):
        @pl.when(owner(t) != pos)
        def _():
            remote(src.at[t], dst.at[pos], ss.at[t], rsem.at[pos], pos_dev(owner(t))).wait_send()

    def tile_recv(src, dst, ss, rsem):
        for q in range(NPOS):
            @pl.when(pos != q)
            def _():
                remote(src.at[0], dst.at[q], ss.at[0], rsem.at[q], pos_dev(q)).wait_recv()


    def field(p, shot, part):
        f = fa[0, p, shot, :, pl.ds(part * NX, NX)].astype(F32)
        prod = jnp.concatenate([rr[p, part * 2, shot], rr[p, part * 2 + 1, shot]], axis=-1)
        return f + prod.astype(F32)

    def b_send(i):
        return remote(bq.at[i], by.at[y], by_s.at[i], by_r.at[y], ((layer // 4) * 4 + i, s))

    def on_others(n, mine, action):
        for i in range(n):
            @pl.when(mine != i)
            def _(i=i):
                action(i)

    for shot in range(2):
        rows = pl.ds(shot * NY, NY)
        if shot == 0:
            r_back(2, 1).wait_recv()
        for k in (2, 3):
            r_back(2, k, shot).wait_recv()
        re, im = field(2, shot, 0), field(2, shot, 1)
        pf2[rows, pl.ds(0, NX)] = re
        pf2[rows, pl.ds(NX, NX)] = im
        for c in range(2):
            i = shot * 2 + c
            cut = slice(c * HALF, (c + 1) * HALF)
            bq[i, :, pl.ds(0, HALF)] = re[:, cut].astype(BF16)
            bq[i, :, pl.ds(HALF, HALF)] = im[:, cut].astype(BF16)

            @pl.when(y != i)
            def _(i=i):
                b_send(i).start()

    by[y] = bq[y]

    loads[3].wait()
    loads[6].wait()
    loads[7].wait()
    for c in t_sends:
        c.wait_recv()
    tr, ti = ty[0, 0], ty[0, 1]
    for j in range(1, 4):
        tr, ti = cmul(ty[j, 0], ty[j, 1], tr, ti)
    tblk[0] = tr
    tblk[1] = ti
    for t in range(NT):
        rt, ct = pl.ds((t // 3) * 16, 16), pl.ds((t % 3) * 128, 128)
        for part in range(2):
            ttile[t, part] = tblk[part, rt, ct]

    for t in range(NT):
        tile_send(t, ttile, ot, tt_s, tt_r)

    def local_iterate(p, slot):
        for shot in range(2):
            rows = pl.ds(shot * NY, NY)
            if p == 2:
                re, im = pf2[rows, pl.ds(0, NX)], pf2[rows, pl.ds(NX, NX)]
            else:
                re, im = field(p, shot, 0), field(p, shot, 1)
            vr, vi = cmul(coef[p, 0], coef[p, 1], re, im)
            va[p + 1, rows, pl.ds(0, NX)] = vr
            va[p + 1, rows, pl.ds(NX, NX)] = vi
            if slot is not None:
                hs[slot, rows, pl.ds(0, NX)] = vr.astype(BF16)
                hs[slot, rows, pl.ds(NX, NX)] = vi.astype(BF16)

    for p in range(LZ):
        coefficients(p)
    local_iterate(2, 0)
    halo_down = remote(hs.at[0], hr.at[0], h_s.at[0], h_r.at[0], up_dev)
    halo_up = remote(hs.at[1], hr.at[1], h_s.at[1], h_r.at[1], dn_dev)

    step(2)

    on_others(4, y, lambda i: remote(bq.at[0], by.at[i], by_s.at[0], by_r.at[i], y_dev(1)).wait_recv())
    re, im = by[0, :, pl.ds(0, HALF)].astype(F32), by[0, :, pl.ds(HALF, HALF)].astype(F32)
    for j in range(1, 4):
        re, im = cmul(ty[j, 0], ty[j, 1], re, im)
        re = re + by[j, :, pl.ds(0, HALF)].astype(F32)
        im = im + by[j, :, pl.ds(HALF, HALF)].astype(F32)
    for t in range(NT):
        rt, ct = slice((t // 3) * 16, (t // 3) * 16 + 16), slice((t % 3) * 128, (t % 3) * 128 + 128)
        tot[t, 0] = re[rt, ct].astype(TT)
        tot[t, 1] = im[rt, ct].astype(TT)
    for t in range(NT):
        tile_send(t, tot, ob, tot_s, tot_r)

    step(3)

    def back(q):
        return remote(ibs.at[q], inb.at[own_tile], ib_s.at[q], ib_r.at[own_tile], pos_dev(q))

    @pl.when(owns)
    def _():
        tile_recv(ttile, ot, tt_s, tt_r)
        tile_recv(tot, ob, tot_s, tot_r)
        cr = jnp.zeros((16, 128), F32)
        ci = jnp.zeros((16, 128), F32)
        for q in range(NPOS):
            ibs[q, 0] = cr.astype(TT)
            ibs[q, 1] = ci.astype(TT)

            @pl.when(pos != q)
            def _():
                back(q).start()

            if q < NPOS - 1:
                cr, ci = cmul(ot[q, 0], ot[q, 1], cr, ci)
                cr = cr + ob[q, 0].astype(F32)
                ci = ci + ob[q, 1].astype(F32)
        inb[own_tile] = ibs[pos]

    md_send(0).wait_recv()
    by_core(lambda c: md_forward(c).start())
    step(4)
    md_forward(0).wait_recv()
    coefficients(LZ)

    def products_in(p):
        r_back(p, 1).wait_recv()
        for shot in range(2):
            for k in (2, 3):
                r_back(p, k, shot).wait_recv()

    products_in(0)
    local_iterate(0, 1)

    for t in range(NT):
        @pl.when(owner(t) != pos)
        def _():
            remote(ibs.at[0], inb.at[t], ib_s.at[0], ib_r.at[t], pos_dev(owner(t))).wait_recv()
    parts = [
        jnp.concatenate(
            [jnp.concatenate([inb[rt * 3 + ct, part] for ct in range(3)], axis=-1) for rt in range(3)], axis=0
        ).astype(F32)
        for part in range(2)
    ]
    re, im = parts
    for j in range(4):
        ins[j, :, pl.ds(0, HALF)] = re.astype(BF16)
        ins[j, :, pl.ds(HALF, HALF)] = im.astype(BF16)
        if j < 3:
            re, im = cmul(ty[j, 0], ty[j, 1], re, im)
            re = re + by[j, :, pl.ds(0, HALF)].astype(F32)
            im = im + by[j, :, pl.ds(HALF, HALF)].astype(F32)

    def in_send(d):
        return remote(ins.at[y_at(d)], inc.at[y], in_s.at[d - 1], in_r.at[d - 1], y_dev(d))

    for d in (1, 2, 3):
        in_send(d).start()
    inc[y] = ins[y]

    step(5)
    halo_down.start()
    halo_up.start()

    products_in(1)
    local_iterate(1, None)

    not_first = jnp.where(layer == 0, 0.0, 1.0).astype(F32)
    not_last = jnp.where(layer == nl - 1, 0.0, 1.0).astype(F32)
    rcols, icols = pl.ds(0, NX), pl.ds(NX, NX)

    for d in (1, 2, 3):
        in_send(d).wait_recv()
    for shot in range(2):
        rows = pl.ds(shot * NY, NY)
        re = jnp.concatenate([inc[shot * 2 + c, :, pl.ds(0, HALF)] for c in range(2)], axis=-1).astype(F32)
        im = jnp.concatenate([inc[shot * 2 + c, :, pl.ds(HALF, HALF)] for c in range(2)], axis=-1).astype(F32)
        vr, vi = cmul(coef[0, 0], coef[0, 1], re, im)
        va[1, rows, rcols] += vr
        va[1, rows, icols] += vi
        nr, ni = cmul(tv[:, rcols], tv[:, icols], re, im)
        nr = nr + pf2[rows, rcols]
        ni = ni + pf2[rows, icols]
        vr, vi = cmul(coef[LZ, 0], coef[LZ, 1], nr, ni)
        va[4, rows, rcols] = vr
        va[4, rows, icols] = vi

    outs = []

    def finish(p):
        for shot in range(2):
            rows = pl.ds(shot * NY, NY)
            diff = []
            for part in range(2):
                cols = pl.ds(part * NX, NX)
                mid = va[p + 1, rows, cols]
                above, below = va[p, rows, cols], va[p + 2, rows, cols]
                if p == 0:
                    above = hr[0, rows, cols].astype(F32) * not_first
                if p == LZ - 1:
                    below = (below + hr[1, rows, cols].astype(F32)) * not_last
                w = mid + 0.5 * (above + below)
                diff.append(lateral(w) - mid)
            dr, di = cmul(coef[p, 0], coef[p, 1], diff[0], diff[1])
            outv[shot, p, :, rcols] = (1.2 * va[p + 1, rows, rcols] + dr * (1.0 / 7.0)).astype(BF16)
            outv[shot, p, :, icols] = (1.2 * va[p + 1, rows, icols] + di * (1.0 / 7.0)).astype(BF16)
            c = pltpu.make_async_copy(outv.at[shot, p], out_hbm.at[shot, p], out_s.at[shot, p])
            c.start()
            outs.append(c)

    finish(1)
    halo_down.wait_recv()
    finish(0)
    halo_up.wait_recv()
    finish(2)

    for p, shot in pieces:
        f_partner(p, shot).wait_send()
        f_forward(p, shot).wait_send()
        for k in (2, 3):
            r_back(p, k, shot).wait_send()
    for p in order:
        f_sibling(p).wait_send()
        r_back(p, 1).wait_send()
    for c in t_sends + [halo_down, halo_up, md_send(0), md_forward(0)]:
        c.wait_send()
    on_others(4, y, lambda i: b_send(i).wait_send())
    for d in (1, 2, 3):
        in_send(d).wait_send()
    for t in range(NT):
        tile_sent(t, ttile, ot, tt_s, tt_r)
        tile_sent(t, tot, ob, tot_s, tot_r)

    @pl.when(owns)
    def _():
        for q in range(NPOS):
            @pl.when(pos != q)
            def _():
                back(q).wait_send()

    for c in outs:
        c.wait()


def on_device(residual_src, src_plane, src_shift, profile, mass, damping, panel, transmission):
    smem = pl.BlockSpec(memory_space=pltpu.SMEM)
    hbm = pl.BlockSpec(memory_space=pltpu.HBM)
    dma = pltpu.SemaphoreType.DMA
    scratch = [
        pltpu.VMEM((2, LZ, NY, W), BF16),
        pltpu.VMEM((2, NY, W), BF16),
        pltpu.VMEM((W, COLS), BF16),
        pltpu.VMEM((4, LZ, 2, NY, W), BF16),
        pltpu.VMEM((4, LZ, 2, NY, COLS), BF16),
        pltpu.VMEM((LZ, 4, 2, NY, COLS), BF16),
        pltpu.VMEM((2, LZ + 1, NY, NX), BF16),
        pltpu.VMEM((LZ + 1, 2, NY, NX), F32),
        pltpu.VMEM((NY, W), F32),
        pltpu.VMEM((4, 2, NY, HALF), F32),
        pltpu.VMEM((2, NY, HALF), F32),
        pltpu.VMEM((NT, 2, 16, 128), F32),
        pltpu.VMEM((NPOS, 2, 16, 128), F32),
        pltpu.VMEM((ROWS, W), F32),
        pltpu.VMEM((4, NY, NX), BF16),
        pltpu.VMEM((4, NY, NX), BF16),
        pltpu.VMEM((NT, 2, 16, 128), TT),
        pltpu.VMEM((NPOS, 2, 16, 128), TT),
        pltpu.VMEM((NPOS, 2, 16, 128), TT),
        pltpu.VMEM((NT, 2, 16, 128), TT),
        pltpu.VMEM((4, NY, NX), BF16),
        pltpu.VMEM((4, NY, NX), BF16),
        pltpu.VMEM((5, ROWS, W), F32),
        pltpu.VMEM((2, ROWS, W), BF16),
        pltpu.VMEM((2, ROWS, W), BF16),
        pltpu.VMEM((2, LZ, NY, W), BF16),
        dma((8,)), dma((LZ, 3, 2)), dma((LZ, 3, 2)), dma((LZ, 3, 2)), dma((LZ, 3, 2)), dma((2,)), dma((2,)),
        dma((3, 2)), dma((3, 2)), dma((NT,)), dma((NPOS,)),
        dma((4,)), dma((4,)), dma((NT,)), dma((NPOS,)), dma((NPOS,)), dma((NT,)),
        dma((3,)), dma((3,)), dma((2,)), dma((2,)), dma((2, LZ)),
    ]
    return pl.pallas_call(
        sweep_kernel,
        out_shape=jax.ShapeDtypeStruct((2, LZ, NY, W), BF16),
        in_specs=[smem] * 2 + [hbm] * 6,
        out_specs=pl.BlockSpec(memory_space=pl.ANY),
        scratch_shapes=scratch,
        name="sweep",
        compiler_params=pltpu.CompilerParams(
            collective_id=0, has_side_effects=True, vmem_limit_bytes=56 * 2**20
        ),
    )(src_plane, src_shift, residual_src, profile, mass, damping, panel, transmission)


def solution(mesh):
    placed = (
        P("shot", "layer", None, None),
        P("shot"),
        P("shot"),
        P("shot", None, None),
        P("layer", None, None),
        P("layer", None, None),
        P("layer", None, "shot"),
        P("layer", None, None),
    )
    return jax.shard_map(
        on_device,
        mesh=mesh,
        in_specs=placed,
        out_specs=P("shot", "layer", None, None),
        check_vma=False,
    )
```
